32 devices in a mesh: groups: 2 (over x), hit: 8 (over z, y), query: 2 (over core).
Axes of the slice: x: 2, y: 2, z: 4, core: 2. Of those that a mesh axis runs over, the one named last changes fastest.
Arguments:
- hits: bfloat16 [16384, 512], P(('groups', 'hit', 'query')), parts along dimension 0, may hold values from -24 to 24
- order: int32 [32, 512], P(('groups', 'hit', 'query')), parts along dimension 0, may hold values from 0 to 511, each once within a row
- valid: int32 [16384], P(('groups', 'hit', 'query')), parts along dimension 0, may hold values 0 or 1
- reach: int32 [16384], P(('groups', 'hit', 'query')), parts along dimension 0, may hold values from 128 to 512, as said below
- enc_wq: bfloat16 [512, 512], replicated, may hold values from -3 to 3
- enc_wk: bfloat16 [512, 512], replicated, may hold values from -1 to 1
- enc_wv: bfloat16 [512, 512], replicated, may hold values from -0.25 to 0.25
- enc_wo: bfloat16 [512, 512], replicated, may hold values from -0.25 to 0.25
- enc_gain1: float32 [512], replicated, may hold values from 0.5 to 1.5
- ffn_up: bfloat16 [512, 2048], replicated, may hold values from -0.25 to 0.25
- ffn_down: bfloat16 [2048, 512], replicated, may hold values from -0.125 to 0.125
- enc_gain2: float32 [512], replicated, may hold values from 0.5 to 1.5
- object_queries: bfloat16 [512, 512], P(('groups', 'hit', 'query')), parts along dimension 0, may hold values from -48 to 48
- dec_wq: bfloat16 [512, 512], replicated, may hold values from -8 to 8
- dec_wk: bfloat16 [512, 512], replicated, may hold values from -0.25 to 0.25
- dec_wv: bfloat16 [512, 512], replicated, may hold values from -0.25 to 0.25
- dec_wo: bfloat16 [512, 512], replicated, may hold values from -0.25 to 0.25
- dec_gain: float32 [512], replicated, may hold values from 0.5 to 1.5
- out_proj: bfloat16 [512, 512], replicated, may hold values from -0.25 to 0.25
Outputs:
- encoded: bfloat16 [16384, 512], P(('groups', 'hit', 'query')), parts along dimension 0
- decoded: bfloat16 [512, 512], P(('groups', 'hit', 'query')), parts along dimension 0
The draws below stay inside these ranges and needn't reach their ends.
There are 2 independent parts, one for each index of `groups`. The reference program is written for one: setup_inputs(seed, part) draws one part's arguments, and reference() takes and returns one part's arrays. A program takes and returns all parts, laid end to end along the dimension named above; an argument that names none is the same for every part. Nothing has to cross between parts.
Inputs may be any that keep to these rules, and one draw needn't show every extreme that they name: The first hit of every block of 512 arrival positions has reach 512.
All inputs are finite; a program needn't handle non-finite values. No bound on the sum of `valid` on one device may be relied on, other than what follows from the above.
Results may differ from the reference program's by a relative error of at most 0.035.
Values may be sent and summed in bfloat16 or wider, within the bound.
A program may use at most 192 MiB of HBM per device.

```python
import math
import jax
import jax.numpy as jnp
from jax import lax

D = 512
HEADS = 8
FF = 2048
WINDOW = 512
HIT_DEV = 512
BLOCKS = 16
HITS = 8192
QUERIES = 256
N_QUERY = 2


def draw_hits(key, part):
    first = jax.random.fold_in(key, 11)
    tracks_per_block = 8
    block_count = HITS // HIT_DEV
    track_centres = jnp.clip(jax.random.normal(jax.random.fold_in(first, 4), (block_count * tracks_per_block, D), jnp.float32), -4.0, 4.0)
    track_ids = jax.random.randint(jax.random.fold_in(first, 5), (HITS,), 0, tracks_per_block, dtype=jnp.int32)
    centre_rows = jnp.arange(HITS, dtype=jnp.int32) // HIT_DEV * tracks_per_block + track_ids
    own_noise = jnp.clip(jax.random.normal(jax.random.fold_in(first, 1), (HITS, D), jnp.float32), -6.0, 6.0)
    base = 0.8 * track_centres[centre_rows] + 0.6 * own_noise
    return base.astype(jnp.bfloat16)


def draw_reach(key, part):
    first = jax.random.fold_in(key, 23)
    drawn = jax.random.randint(first, (HITS,), WINDOW // 4, WINDOW + 1, dtype=jnp.int32)
    head = jnp.arange(HITS, dtype=jnp.int32) % HIT_DEV == 0
    return jnp.where(head, WINDOW, drawn).astype(jnp.int32)


def encoder_pair(key):
    first = jax.random.fold_in(key, 37)
    wk = jnp.clip(jax.random.normal(jax.random.fold_in(first, 1), (D, D), jnp.float32), -4.0, 4.0) / math.sqrt(D)
    noise = jnp.clip(jax.random.normal(jax.random.fold_in(first, 2), (D, D), jnp.float32), -4.0, 4.0) / math.sqrt(D)
    wq = noise
    return (wq, wk)


def draw_enc_wq(key, part):
    return encoder_pair(key)[0].astype(jnp.bfloat16)


def draw_enc_wk(key, part):
    return encoder_pair(key)[1].astype(jnp.bfloat16)


def draw_object_queries(key, part):
    first = jax.random.fold_in(key, 41)
    base = jnp.clip(jax.random.normal(jax.random.fold_in(first, 1), (QUERIES, D), jnp.float32), -6.0, 6.0)
    base = base * 0.125
    return base.astype(jnp.bfloat16)


def draw_dec_wq(key, part):
    first = jax.random.fold_in(key, 53)
    base = jnp.clip(jax.random.normal(first, (D, D), jnp.float32), -4.0, 4.0) * (16.0 / math.sqrt(D))
    return base.astype(jnp.bfloat16)


def with_ends(result, stream_key, low, high):
    spot = [jax.random.randint(jax.random.fold_in(stream_key, axis), (), 0, length) for axis, length in enumerate(result.shape)]
    widest = result.shape.index(max(result.shape))
    beside = spot[:widest] + [(spot[widest] + 1) % result.shape[widest]] + spot[widest + 1:]
    return result.at[tuple(spot)].set(low).at[tuple(beside)].set(high)


def bell_draw(stream_key, extent, scale, limit, kind=jnp.bfloat16):
    values = scale * jax.random.normal(stream_key, extent, jnp.float32)
    return jnp.clip(values, min=-limit, max=limit).astype(kind)


def setup_inputs(seed: int = 0, part: int = 0) -> dict:
    streams_of = jax.random.split(jax.random.key(seed), 20)
    own_keys = jax.random.split(jax.random.fold_in(streams_of[19], part), 20)
    return {
        "hits": draw_hits(jax.random.fold_in(jax.random.fold_in(streams_of[19], part), 71), part),
        "order": jax.vmap(lambda own: jax.random.permutation(own, HIT_DEV))(jax.random.split(own_keys[1], BLOCKS)).reshape((BLOCKS, HIT_DEV)).astype(jnp.int32),
        "valid": with_ends((jax.random.randint(own_keys[2], (HITS,), 0, 4) < 3).astype(jnp.int32), jax.random.fold_in(own_keys[2], 1), 0, 1),
        "reach": draw_reach(jax.random.fold_in(jax.random.fold_in(streams_of[19], part), 71), part),
        "enc_wq": draw_enc_wq(jax.random.fold_in(streams_of[19], 71), part),
        "enc_wk": draw_enc_wk(jax.random.fold_in(streams_of[19], 71), part),
        "enc_wv": bell_draw(streams_of[6], (D, D), D ** -0.5, 0.25),
        "enc_wo": bell_draw(streams_of[7], (D, D), D ** -0.5, 0.25),
        "enc_gain1": jnp.clip(1.0 + 0.1 * jax.random.normal(streams_of[8], (D,), jnp.float32), 0.5, 1.5),
        "ffn_up": bell_draw(streams_of[9], (D, FF), D ** -0.5, 0.25),
        "ffn_down": bell_draw(streams_of[10], (FF, D), FF ** -0.5, 0.125),
        "enc_gain2": jnp.clip(1.0 + 0.1 * jax.random.normal(streams_of[11], (D,), jnp.float32), 0.5, 1.5),
        "object_queries": draw_object_queries(jax.random.fold_in(jax.random.fold_in(streams_of[19], part), 71), part),
        "dec_wq": draw_dec_wq(jax.random.fold_in(streams_of[19], 71), part),
        "dec_wk": bell_draw(streams_of[14], (D, D), D ** -0.5, 0.25),
        "dec_wv": bell_draw(streams_of[15], (D, D), D ** -0.5, 0.25),
        "dec_wo": bell_draw(streams_of[16], (D, D), D ** -0.5, 0.25),
        "dec_gain": jnp.clip(1.0 + 0.1 * jax.random.normal(streams_of[17], (D,), jnp.float32), 0.5, 1.5),
        "out_proj": bell_draw(streams_of[18], (D, D), D ** -0.5, 0.25),
    }


def project(rows, weight):
    return jnp.dot(rows, weight, preferred_element_type=jnp.float32).astype(jnp.bfloat16)

def rms_norm(values, gain):
    scale = lax.rsqrt(lax.optimization_barrier(jnp.mean(values * values, axis=-1, keepdims=True)) + 1e-05)
    return values * scale * gain.astype(jnp.float32)

def band_attention(queries, keys, values, key_valid, reach):
    count = queries.shape[0]
    span = keys.shape[0]
    margin = (span - count) // 2
    width = queries.shape[1] // HEADS
    query_heads = queries.reshape(count, HEADS, width).astype(jnp.float32)
    key_heads = keys.reshape(span, HEADS, width).astype(jnp.float32)
    value_heads = values.reshape(span, HEADS, width).astype(jnp.float32)
    scores = jnp.einsum('qhd,khd->hqk', query_heads, key_heads) * (1.0 / math.sqrt(width))
    offset = jnp.arange(span, dtype=jnp.int32)[None, :] - (jnp.arange(count, dtype=jnp.int32)[:, None] + margin)
    allowed = (jnp.abs(offset) <= reach[:, None]) & ((key_valid[None, :] > 0) | (offset == 0))
    scores = jnp.where(allowed[None], scores, -jnp.inf)
    peak = lax.optimization_barrier(jnp.max(scores, axis=2, keepdims=True))
    expo = jnp.where(allowed[None], jnp.exp(scores - peak), 0.0)
    probs = (expo / lax.optimization_barrier(jnp.sum(expo, axis=2, keepdims=True))).astype(jnp.bfloat16)
    context = jnp.einsum('hqk,khd->qhd', probs.astype(jnp.float32), value_heads)
    return context.reshape(count, HEADS * width).astype(jnp.bfloat16)

def encoder_tail(context, sorted_hits, enc_wo, enc_gain1, ffn_up, ffn_down, enc_gain2):
    attn_res = jnp.dot(context, enc_wo, preferred_element_type=jnp.float32) + sorted_hits.astype(jnp.float32)
    middle = rms_norm(attn_res, enc_gain1).astype(jnp.bfloat16)
    hidden = jax.nn.gelu(jnp.dot(middle, ffn_up, preferred_element_type=jnp.float32), approximate=True).astype(jnp.bfloat16)
    ffn_res = jnp.dot(hidden, ffn_down, preferred_element_type=jnp.float32) + middle.astype(jnp.float32)
    return rms_norm(ffn_res, enc_gain2).astype(jnp.bfloat16)

def span_partial(queries, keys, values):
    count = queries.shape[0]
    span = keys.shape[0]
    width = queries.shape[1] // HEADS
    query_heads = queries.reshape(count, HEADS, width).astype(jnp.float32)
    key_heads = keys.reshape(span, HEADS, width).astype(jnp.float32)
    value_heads = values.reshape(span, HEADS, width).astype(jnp.float32)
    scores = jnp.einsum('qhd,khd->qhk', query_heads, key_heads) * (1.0 / math.sqrt(width))
    peak = lax.optimization_barrier(jnp.max(scores, axis=2))
    expo = jnp.exp(scores - peak[:, :, None])
    total = lax.optimization_barrier(jnp.sum(expo, axis=2))
    weights = expo.astype(jnp.bfloat16)
    output = jnp.einsum('qhk,khd->qhd', weights.astype(jnp.float32), value_heads)
    return (peak, total, output.reshape(count, HEADS * width))

def reference(hits, order, valid, reach, enc_wq, enc_wk, enc_wv, enc_wo, enc_gain1, ffn_up, ffn_down, enc_gain2, object_queries, dec_wq, dec_wk, dec_wv, dec_wo, dec_gain, out_proj):
    nblocks = order.shape[0]
    per_block = order.shape[1]
    place = (jnp.arange(nblocks, dtype=jnp.int32)[:, None] * per_block + order.astype(jnp.int32)).reshape(-1)
    sorted_hits = hits[place]
    sorted_valid = valid[place]
    sorted_reach = reach[place]
    total_hits = sorted_hits.shape[0]
    queries = project(sorted_hits, enc_wq)
    keys = project(sorted_hits, enc_wk)
    values = project(sorted_hits, enc_wv)
    wide_keys = jnp.concatenate([keys[total_hits - WINDOW:], keys, keys[:WINDOW]], axis=0)
    wide_values = jnp.concatenate([values[total_hits - WINDOW:], values, values[:WINDOW]], axis=0)
    wide_valid = jnp.concatenate([sorted_valid[total_hits - WINDOW:], sorted_valid, sorted_valid[:WINDOW]], axis=0)
    block = 512 if per_block % 512 == 0 else per_block

    def attend(index):
        start = index * block
        return band_attention(lax.dynamic_slice_in_dim(queries, start, block, 0), lax.dynamic_slice_in_dim(wide_keys, start, block + 2 * WINDOW, 0), lax.dynamic_slice_in_dim(wide_values, start, block + 2 * WINDOW, 0), lax.dynamic_slice_in_dim(wide_valid, start, block + 2 * WINDOW, 0), lax.dynamic_slice_in_dim(sorted_reach, start, block, 0))
    context = lax.map(attend, jnp.arange(total_hits // block, dtype=jnp.int32)).reshape(total_hits, D)
    encoded = encoder_tail(context, sorted_hits, enc_wo, enc_gain1, ffn_up, ffn_down, enc_gain2)
    dec_queries = project(object_queries, dec_wq)
    dec_keys = project(encoded, dec_wk)
    dec_values = project(encoded, dec_wv)
    span = per_block * N_QUERY

    def one_span(index):
        start = index * span
        return span_partial(dec_queries, lax.dynamic_slice_in_dim(dec_keys, start, span, 0), lax.dynamic_slice_in_dim(dec_values, start, span, 0))
    peaks, totals, outputs = lax.map(one_span, jnp.arange(total_hits // span, dtype=jnp.int32))
    width = D // HEADS
    top = lax.optimization_barrier(jnp.max(peaks, axis=0))
    factor = jnp.exp(peaks - top[None])
    denom = lax.optimization_barrier(jnp.sum(totals * factor, axis=0))
    numer = lax.optimization_barrier(jnp.sum(outputs * jnp.repeat(factor, width, axis=2), axis=0))
    cross = (numer / jnp.repeat(denom, width, axis=1)).astype(jnp.bfloat16)
    dec_res = jnp.dot(cross, dec_wo, preferred_element_type=jnp.float32) + object_queries.astype(jnp.float32)
    normed = rms_norm(dec_res, dec_gain).astype(jnp.bfloat16)
    decoded = jnp.dot(normed, out_proj, preferred_element_type=jnp.float32).astype(jnp.bfloat16)
    return (encoded, decoded)
```

```python
import functools
import math

import jax
import jax.numpy as jnp
from jax import lax
from jax.experimental import pallas as pl
from jax.experimental.pallas import tpu as pltpu
from jax.sharding import PartitionSpec as P

HEADS = 8
LANES = 128
TAIL = 16
MESH = pl.DeviceIdType.MESH
BF16 = jnp.bfloat16
F32 = jnp.float32
FAR = -1e30
NT = (((1,), (1,)), ((), ()))


def dot(a, b):
    return jnp.dot(a, b, preferred_element_type=F32)


def dot_nt(a, b):
    return lax.dot_general(a, b, NT, preferred_element_type=F32)


def rms_norm(values, gain):
    scale = lax.rsqrt(jnp.mean(values * values, axis=-1, keepdims=True) + 1e-05)
    return values * scale * gain


def gelu(x):
    inner = math.sqrt(2.0 / math.pi) * (x + 0.044715 * (x * x * x))
    return 0.5 * x * (1.0 + jnp.tanh(inner))


def kernel(
    n_hit,
    n_query,
    order_ref,
    valid_ref,
    reach_ref,
    gain1_ref,
    gain2_ref,
    dgain_ref,
    objq_ref,
    hits_hbm,
    wq_hbm,
    wk_hbm,
    wv_hbm,
    dwq_hbm,
    wo_hbm,
    up_hbm,
    down_hbm,
    dwk_hbm,
    dwv_hbm,
    dwo_hbm,
    out_hbm,
    enc_hbm,
    dec_ref,
    hits_s,
    wq_s,
    wk_s,
    wv_s,
    dwq_s,
    wo_s,
    up_s,
    down_s,
    dwk_s,
    dwv_s,
    dwo_s,
    out_s,
    ext_s,
    halo_s,
    q_s,
    k_s,
    v_s,
    bias_s,
    acc_s,
    mx_s,
    ctx_s,
    ffn_s,
    enc_s,
    dk_s,
    dv_s,
    qall_s,
    o_s,
    lse_s,
    pair_s,
    pairin_s,
    msg_s,
    msgin_s,
    load_sem,
    halo_send,
    halo_recv,
    dq_send,
    dq_recv,
    pair_send,
    pair_recv,
    msg_send,
    msg_recv,
    enc_sem,
):
    group = lax.axis_index("groups")
    hit = lax.axis_index("hit")
    core = lax.axis_index("query")
    count = n_hit * n_query
    me = hit * n_query + core
    n, width = hits_s.shape
    half = n // 2
    pairs = width // LANES
    head_width = width // HEADS
    owned = objq_ref.shape[0]
    part = n_hit * owned
    factor = math.log2(math.e) / math.sqrt(head_width)

    loads = [
        pltpu.make_async_copy(source, target, load_sem.at[i])
        for i, (source, target) in enumerate(
            (
                (hits_hbm, hits_s),
                (dwq_hbm, dwq_s),
                (wq_hbm, wq_s),
                (wk_hbm, wk_s),
                (wv_hbm, wv_s),
                (wo_hbm, wo_s),
                (up_hbm, up_s),
                (down_hbm, down_s),
                (dwk_hbm, dwk_s),
                (dwv_hbm, dwv_s),
                (dwo_hbm, dwo_s),
                (out_hbm, out_s),
            )
        )
    ]
    for load in loads:
        load.start()

    def device(block):
        return (group, lax.div(block, n_query), lax.rem(block, n_query))

    barrier = pltpu.get_barrier_semaphore()

    def greet(d, carry):
        pl.semaphore_signal(
            barrier, inc=1, device_id=device(lax.rem(me + d, count)), device_id_type=MESH
        )
        return carry

    lax.fori_loop(1, count, greet, 0)

    order_rows = jnp.broadcast_to(order_ref[...].astype(F32), (LANES, n))
    order_col = jnp.transpose(order_rows)[:, :1].astype(jnp.int32)
    hot = lax.broadcasted_iota(jnp.int32, (n, n), 1) == order_col
    onehot = jnp.where(hot, 1.0, 0.0)
    reach_col = jnp.sum(onehot * reach_ref[...].astype(F32), axis=1, keepdims=True)
    onehot = onehot.astype(BF16)
    valid_rows = jnp.broadcast_to(valid_ref[...].astype(F32), (TAIL, n)).astype(BF16)
    sorted_valid = dot_nt(valid_rows, onehot)
    ext_s[pl.ds(n, TAIL), :] = sorted_valid.astype(BF16)
    loads[0].wait()
    ext_s[pl.ds(0, n), :] = dot(onehot, hits_s[...]).astype(BF16)

    pl.semaphore_wait(barrier, count - 1)

    right = lax.rem(me + 1, count)
    left = lax.rem(me + count - 1, count)
    halo = []
    for side, target in ((0, right), (1, left)):
        copy = pltpu.make_async_remote_copy(
            src_ref=ext_s,
            dst_ref=halo_s.at[side],
            send_sem=halo_send.at[side],
            recv_sem=halo_recv.at[side],
            device_id=device(target),
            device_id_type=MESH,
        )
        copy.start()
        halo.append(copy)

    loads[1].wait()
    my_slot = core * n_hit + hit
    qall_s[my_slot] = (dot(objq_ref[...], dwq_s[...]) * factor).astype(BF16)

    def dq_copy(d):
        peer = lax.rem(me + d, count)
        return pltpu.make_async_remote_copy(
            src_ref=qall_s.at[my_slot],
            dst_ref=qall_s.at[my_slot],
            send_sem=dq_send.at[d],
            recv_sem=dq_recv.at[my_slot],
            device_id=device(peer),
            device_id_type=MESH,
        )

    def dq_start(d, carry):
        dq_copy(d).start()
        return carry

    lax.fori_loop(1, count, dq_start, 0)

    for load in loads[2:5]:
        load.wait()
    own = pl.ds(n, n)
    rows = ext_s[pl.ds(0, n), :]
    q_s[...] = (dot(rows, wq_s[...]) * factor).astype(BF16)
    k_s[own, :] = dot(rows, wk_s[...]).astype(BF16)
    v_s[own, :] = dot(rows, wv_s[...]).astype(BF16)

    def bias_of(place, valid_row):
        offset = (
            lax.broadcasted_iota(jnp.int32, (n, n), 1)
            - lax.broadcasted_iota(jnp.int32, (n, n), 0)
            + (place - 1) * n
        )
        far = jnp.abs(offset).astype(F32) > reach_col
        gone = (valid_row < 0.5) & (offset != 0)
        bias_s[:, pl.ds(place * n, n)] = jnp.where(far | gone, FAR, 0.0)

    bias_of(1, sorted_valid[:1, :])

    lane = lax.broadcasted_iota(jnp.int32, (1, LANES), 1)
    first = jnp.where(lane < head_width, 1.0, 0.0)
    keep = (first.astype(BF16), (1.0 - first).astype(BF16))

    def own_pair(p, carry):
        cols = pl.ds(pl.multiple_of(p * LANES, LANES), LANES)
        qp, kp, vp = q_s[:, cols], k_s[own, cols], v_s[own, cols]
        for h in range(2):
            s = dot_nt(qp * keep[h], kp) + bias_s[:, own]
            m = jnp.max(s, axis=1, keepdims=True)
            weights = jnp.exp2(s - m).astype(BF16)
            acc_s[p, h] = dot(weights, vp * keep[h] + keep[1 - h])
            mx_s[p, h] = jnp.broadcast_to(m, (n, LANES))
        return carry

    lax.fori_loop(0, pairs, own_pair, 0)

    for side in range(2):
        halo[side].wait_recv()
        there = pl.ds(2 * side * n, n)
        rows = halo_s[side, pl.ds(0, n), :]
        k_s[there, :] = dot(rows, wk_s[...]).astype(BF16)
        v_s[there, :] = dot(rows, wv_s[...]).astype(BF16)
        bias_of(2 * side, halo_s[side, pl.ds(n, TAIL), :].astype(F32)[:1, :])

    def split_heads(o0, o1):
        front = lane < head_width
        return (
            jnp.where(front, o0, o1),
            pltpu.roll(jnp.where(front, o1, o0), head_width, 1),
        )

    def wide_pair(p, carry):
        cols = pl.ds(pl.multiple_of(p * LANES, LANES), LANES)
        for tile, spans in (
            (0, (pl.ds(0, n), pl.ds(2 * n, half))),
            (1, (pl.ds(half, half), pl.ds(2 * n, n))),
        ):
            here = pl.ds(tile * half, half)
            qp = q_s[here, cols]
            outs = []
            for h in range(2):
                qh = qp * keep[h]
                scores = [dot_nt(qh, k_s[span, cols]) + bias_s[here, span] for span in spans]
                before = mx_s[p, h, here, :]
                m = before[:, :1]
                for s in scores:
                    m = jnp.maximum(m, jnp.max(s, axis=1, keepdims=True))
                out = acc_s[p, h, here, :] * jnp.exp2(before - m)
                for s, span in zip(scores, spans):
                    out += dot(
                        jnp.exp2(s - m).astype(BF16), v_s[span, cols] * keep[h] + keep[1 - h]
                    )
                outs.append(out)
            value, total = split_heads(*outs)
            ctx_s[here, cols] = (value / total).astype(BF16)
        return carry

    lax.fori_loop(0, pairs, wide_pair, 0)

    for load in loads[5:8]:
        load.wait()
    middle = rms_norm(
        dot(ctx_s[...], wo_s[...]) + ext_s[pl.ds(0, n), :].astype(F32), gain1_ref[...]
    ).astype(BF16)
    ffn_s[...] = middle.astype(F32)
    hidden_width = up_s.shape[1]
    step = 512

    for c in range(hidden_width // step):
        hidden = gelu(dot(middle, up_s[:, pl.ds(c * step, step)])).astype(BF16)
        ffn_s[...] += dot(hidden, down_s[pl.ds(c * step, step), :])
    encoded = rms_norm(ffn_s[...], gain2_ref[...]).astype(BF16)
    enc_s[...] = encoded
    enc_copy = pltpu.make_async_copy(enc_s, enc_hbm, enc_sem)
    enc_copy.start()

    loads[8].wait()
    loads[9].wait()
    dk_s[...] = dot(encoded, dwk_s[...]).astype(BF16)
    dv_s[...] = dot(encoded, dwv_s[...]).astype(BF16)

    def dq_wait(d, carry):
        peer = lax.rem(me + d, count)
        slot = lax.rem(peer, n_query) * n_hit + lax.div(peer, n_query)
        pltpu.make_async_remote_copy(
            src_ref=qall_s.at[slot],
            dst_ref=qall_s.at[slot],
            send_sem=dq_send.at[d],
            recv_sem=dq_recv.at[slot],
            device_id=device(peer),
            device_id_type=MESH,
        ).wait_recv()
        return carry

    lax.fori_loop(1, count, dq_wait, 0)

    def partial(which):
        slots = pl.ds(which * n_hit, n_hit)

        for p in range(pairs):
            cols = pl.ds(p * LANES, LANES)
            qp = qall_s[slots, :, cols].reshape(part, LANES)
            kp, vp = dk_s[:, cols], dv_s[:, cols]
            outs, tops = [], []
            for h in range(2):
                s = dot_nt(qp * keep[h], kp)
                m = jnp.max(s, axis=1, keepdims=True)
                outs.append(dot(jnp.exp2(s - m).astype(BF16), vp * keep[h] + keep[1 - h]))
                tops.append(m)
            value, total = split_heads(*outs)
            o_s[:, cols] = value / total
            lse_s[:, cols] = jnp.where(lane < head_width, tops[0], tops[1]) + jnp.log2(total)

    column = lax.broadcasted_iota(jnp.int32, (width, LANES), 0)
    slot_of = lax.broadcasted_iota(jnp.int32, (width, LANES), 1)

    def packed(lse):
        total = jnp.zeros((lse.shape[0], LANES), F32)
        rest = lse
        for k in range(3):
            term = rest.astype(BF16)
            rest = rest - term.astype(F32)
            pick = jnp.where(column == (slot_of - k * HEADS) * head_width, 1.0, 0.0)
            total += dot(term, pick.astype(BF16))
        return total.astype(BF16)

    spread_row = lax.broadcasted_iota(jnp.int32, (LANES, width), 0)
    spread_col = lax.broadcasted_iota(jnp.int32, (LANES, width), 1)
    spread = jnp.zeros((LANES, width), F32)
    for k in range(3):
        low = (spread_row - k * HEADS) * head_width
        spread += jnp.where((spread_col >= low) & (spread_col < low + head_width), 1.0, 0.0)
    spread = spread.astype(BF16)

    partial(1 - core)
    pair_s[:, pl.ds(0, width)] = o_s[...].astype(BF16)
    pair_s[:, pl.ds(width, LANES)] = packed(lse_s[...])
    pair_copy = pltpu.make_async_remote_copy(
        src_ref=pair_s,
        dst_ref=pairin_s,
        send_sem=pair_send,
        recv_sem=pair_recv,
        device_id=(group, hit, 1 - core),
        device_id_type=MESH,
    )
    pair_copy.start()
    partial(core)
    pair_copy.wait_recv()
    lse_a, lse_b = lse_s[...], dot(pairin_s[:, pl.ds(width, LANES)], spread)
    top = jnp.maximum(lse_a, lse_b)
    wa, wb = jnp.exp2(lse_a - top), jnp.exp2(lse_b - top)
    total = wa + wb
    merged = (wa * o_s[...] + wb * pairin_s[:, pl.ds(0, width)].astype(F32)) / total
    msg_s[:, :, pl.ds(0, width)] = merged.astype(BF16).reshape(n_hit, owned, width)
    msg_s[:, :, pl.ds(width, LANES)] = packed(top + jnp.log2(total)).reshape(
        n_hit, owned, LANES
    )

    def msg_copy(d):
        peer = lax.rem(hit + d, n_hit)
        return pltpu.make_async_remote_copy(
            src_ref=msg_s.at[peer],
            dst_ref=msgin_s.at[hit],
            send_sem=msg_send.at[d],
            recv_sem=msg_recv.at[hit],
            device_id=(group, peer, core),
            device_id_type=MESH,
        )

    def msg_start(d, carry):
        msg_copy(d).start()
        return carry

    lax.fori_loop(1, n_hit, msg_start, 0)
    msgin_s[hit] = msg_s[hit]
    loads[10].wait()
    loads[11].wait()

    def msg_wait(d, carry):
        peer = lax.rem(hit + d, n_hit)
        pltpu.make_async_remote_copy(
            src_ref=msg_s.at[peer],
            dst_ref=msgin_s.at[peer],
            send_sem=msg_send.at[d],
            recv_sem=msg_recv.at[peer],
            device_id=(group, peer, core),
            device_id_type=MESH,
        ).wait_recv()
        return carry

    lax.fori_loop(1, n_hit, msg_wait, 0)
    values = msgin_s[:, :, pl.ds(0, width)].astype(F32)
    lse = dot(msgin_s[:, :, pl.ds(width, LANES)].reshape(part, LANES), spread)
    lse = lse.reshape(n_hit, owned, width)
    weights = jnp.exp2(lse - jnp.max(lse, axis=0, keepdims=True))
    cross = jnp.sum(weights * values, axis=0) / jnp.sum(weights, axis=0)
    res = dot(cross.astype(BF16), dwo_s[...]) + objq_ref[...].astype(F32)
    normed = rms_norm(res, dgain_ref[...]).astype(BF16)
    dec_ref[...] = dot(normed, out_s[...]).astype(BF16)

    for copy in halo:
        copy.wait_send()

    def dq_sent(d, carry):
        dq_copy(d).wait_send()
        return carry

    lax.fori_loop(1, count, dq_sent, 0)
    pair_copy.wait_send()

    def msg_sent(d, carry):
        msg_copy(d).wait_send()
        return carry

    lax.fori_loop(1, n_hit, msg_sent, 0)
    enc_copy.wait()


def on_device(
    n_hit,
    n_query,
    hits,
    order,
    valid,
    reach,
    enc_wq,
    enc_wk,
    enc_wv,
    enc_wo,
    enc_gain1,
    ffn_up,
    ffn_down,
    enc_gain2,
    object_queries,
    dec_wq,
    dec_wk,
    dec_wv,
    dec_wo,
    dec_gain,
    out_proj,
):
    n, width = hits.shape
    owned = object_queries.shape[0]
    hidden = ffn_up.shape[1]
    count = n_hit * n_query
    part = n_hit * owned
    pairs = width // LANES
    vmem = pl.BlockSpec(memory_space=pltpu.VMEM)
    anywhere = pl.BlockSpec(memory_space=pl.ANY)
    square = pltpu.VMEM((width, width), BF16)
    dma = pltpu.SemaphoreType.DMA
    return pl.pallas_call(
        functools.partial(kernel, n_hit, n_query),
        out_shape=(
            jax.ShapeDtypeStruct((n, width), BF16),
            jax.ShapeDtypeStruct((owned, width), BF16),
        ),
        in_specs=[vmem] * 7 + [anywhere] * 12,
        out_specs=(anywhere, vmem),
        scratch_shapes=[
            pltpu.VMEM((n, width), BF16),
            square,
            square,
            square,
            square,
            square,
            pltpu.VMEM((width, hidden), BF16),
            pltpu.VMEM((hidden, width), BF16),
            square,
            square,
            square,
            square,
            pltpu.VMEM((n + TAIL, width), BF16),
            pltpu.VMEM((2, n + TAIL, width), BF16),
            pltpu.VMEM((n, width), BF16),
            pltpu.VMEM((3 * n, width), BF16),
            pltpu.VMEM((3 * n, width), BF16),
            pltpu.VMEM((n, 3 * n), F32),
            pltpu.VMEM((pairs, 2, n, LANES), F32),
            pltpu.VMEM((pairs, 2, n, LANES), F32),
            pltpu.VMEM((n, width), BF16),
            pltpu.VMEM((n, width), F32),
            pltpu.VMEM((n, width), BF16),
            pltpu.VMEM((n, width), BF16),
            pltpu.VMEM((n, width), BF16),
            pltpu.VMEM((count, owned, width), BF16),
            pltpu.VMEM((part, width), F32),
            pltpu.VMEM((part, width), F32),
            pltpu.VMEM((part, width + LANES), BF16),
            pltpu.VMEM((part, width + LANES), BF16),
            pltpu.VMEM((n_hit, owned, width + LANES), BF16),
            pltpu.VMEM((n_hit, owned, width + LANES), BF16),
            dma((12,)),
            dma((2,)),
            dma((2,)),
            dma((count,)),
            dma((count,)),
            dma,
            dma,
            dma((n_hit,)),
            dma((n_hit,)),
            dma,
        ],
        compiler_params=pltpu.CompilerParams(
            collective_id=0, has_side_effects=True, vmem_limit_bytes=56 * 1024 * 1024
        ),
        name="track",
    )(
        order,
        valid.reshape(1, n),
        reach.reshape(1, n),
        enc_gain1.reshape(1, width),
        enc_gain2.reshape(1, width),
        dec_gain.reshape(1, width),
        object_queries,
        hits,
        enc_wq,
        enc_wk,
        enc_wv,
        dec_wq,
        enc_wo,
        ffn_up,
        ffn_down,
        dec_wk,
        dec_wv,
        dec_wo,
        out_proj,
    )


def solution(mesh):
    split = P(("groups", "hit", "query"), None)
    flat = P(("groups", "hit", "query"))
    in_specs = (split, split, flat, flat) + (P(),) * 8 + (split,) + (P(),) * 6
    return jax.shard_map(
        functools.partial(on_device, mesh.shape["hit"], mesh.shape["query"]),
        mesh=mesh,
        in_specs=in_specs,
        out_specs=(split, split),
        check_vma=False,
    )
```

```python
import functools
import math

import jax
import jax.numpy as jnp
from jax import lax
from jax.experimental import pallas as pl
from jax.experimental.pallas import tpu as pltpu
from jax.sharding import PartitionSpec as P

HEADS = 8
LANES = 128
TAIL = 16
MESH = pl.DeviceIdType.MESH
BF16 = jnp.bfloat16
F32 = jnp.float32
FAR = -1e30
NT = (((1,), (1,)), ((), ()))


def dot(a, b):
    return jnp.dot(a, b, preferred_element_type=F32)


def dot_nt(a, b):
    return lax.dot_general(a, b, NT, preferred_element_type=F32)


def rms_norm(values, gain):
    scale = lax.rsqrt(jnp.mean(values * values, axis=-1, keepdims=True) + 1e-05)
    return values * scale * gain


def gelu(x):
    inner = math.sqrt(2.0 / math.pi) * (x + 0.044715 * (x * x * x))
    return 0.5 * x * (1.0 + jnp.tanh(inner))


def kernel(
    n_hit,
    n_query,
    order_ref,
    valid_ref,
    reach_ref,
    gain1_ref,
    gain2_ref,
    dgain_ref,
    objq_ref,
    hits_hbm,
    wq_hbm,
    wk_hbm,
    wv_hbm,
    dwq_hbm,
    wo_hbm,
    up_hbm,
    down_hbm,
    dwk_hbm,
    dwv_hbm,
    dwo_hbm,
    out_hbm,
    enc_hbm,
    dec_ref,
    hits_s,
    wq_s,
    wk_s,
    wv_s,
    dwq_s,
    wo_s,
    up_s,
    down_s,
    dwk_s,
    dwv_s,
    dwo_s,
    out_s,
    ext_s,
    halo_s,
    q_s,
    k_s,
    v_s,
    bias_s,
    acc_s,
    mx_s,
    ctx_s,
    ffn_s,
    enc_s,
    dk_s,
    dv_s,
    qall_s,
    o_s,
    lse_s,
    pair_s,
    pairin_s,
    msg_s,
    msgin_s,
    load_sem,
    halo_send,
    halo_recv,
    dq_send,
    dq_recv,
    pair_send,
    pair_recv,
    msg_send,
    msg_recv,
    enc_sem,
):
    group = lax.axis_index("groups")
    hit = lax.axis_index("hit")
    core = lax.axis_index("query")
    count = n_hit * n_query
    me = hit * n_query + core
    n, width = hits_s.shape
    half = n // 2
    pairs = width // LANES
    head_width = width // HEADS
    owned = objq_ref.shape[0]
    part = n_hit * owned
    factor = math.log2(math.e) / math.sqrt(head_width)

    loads = [
        pltpu.make_async_copy(source, target, load_sem.at[i])
        for i, (source, target) in enumerate(
            (
                (hits_hbm, hits_s),
                (dwq_hbm, dwq_s),
                (wq_hbm, wq_s),
                (wk_hbm, wk_s),
                (wv_hbm, wv_s),
                (wo_hbm, wo_s),
                (up_hbm, up_s),
                (down_hbm, down_s),
                (dwk_hbm, dwk_s),
                (dwv_hbm, dwv_s),
                (dwo_hbm, dwo_s),
                (out_hbm, out_s),
            )
        )
    ]
    for load in loads:
        load.start()

    def device(block):
        return (group, lax.div(block, n_query), lax.rem(block, n_query))

    barrier = pltpu.get_barrier_semaphore()

    def greet(d, carry):
        pl.semaphore_signal(
            barrier, inc=1, device_id=device(lax.rem(me + d, count)), device_id_type=MESH
        )
        return carry

    lax.fori_loop(1, count, greet, 0)

    order_rows = jnp.broadcast_to(order_ref[...].astype(F32), (LANES, n))
    order_col = jnp.transpose(order_rows)[:, :1].astype(jnp.int32)
    hot = lax.broadcasted_iota(jnp.int32, (n, n), 1) == order_col
    onehot = jnp.where(hot, 1.0, 0.0)
    reach_col = jnp.sum(onehot * reach_ref[...].astype(F32), axis=1, keepdims=True)
    onehot = onehot.astype(BF16)
    valid_rows = jnp.broadcast_to(valid_ref[...].astype(F32), (TAIL, n)).astype(BF16)
    sorted_valid = dot_nt(valid_rows, onehot)
    ext_s[pl.ds(0, TAIL), :] = sorted_valid.astype(BF16)
    ext_s[pl.ds(n + TAIL, TAIL), :] = sorted_valid.astype(BF16)
    loads[0].wait()
    ext_s[pl.ds(TAIL, n), :] = dot(onehot, hits_s[...]).astype(BF16)

    pl.semaphore_wait(barrier, count - 1)

    near_side, far_side = 1 - core, core
    far_block = lax.rem(me + count - 1 + 2 * core, count)
    piece = half + TAIL

    def near_copy(side):
        return pltpu.make_async_remote_copy(
            src_ref=ext_s,
            dst_ref=halo_s.at[side],
            send_sem=halo_send.at[0],
            recv_sem=halo_recv.at[0],
            device_id=(group, hit, 1 - core),
            device_id_type=MESH,
        )

    def far_copy(side, k):
        if k == 0:
            span = pl.ds(pl.multiple_of((1 - side) * piece, TAIL), piece)
        else:
            span = pl.ds(pl.multiple_of(TAIL + side * half, TAIL), half)
        return pltpu.make_async_remote_copy(
            src_ref=ext_s.at[span],
            dst_ref=halo_s.at[side, span],
            send_sem=halo_send.at[1 + k],
            recv_sem=halo_recv.at[1 + k],
            device_id=device(far_block),
            device_id_type=MESH,
        )

    far_copy(1 - core, 0).start()
    far_copy(1 - core, 1).start()
    near_copy(core).start()

    loads[1].wait()
    my_slot = core * n_hit + hit
    qall_s[my_slot] = (dot(objq_ref[...], dwq_s[...]) * factor).astype(BF16)

    def dq_copy(d):
        peer = lax.rem(me + d, count)
        return pltpu.make_async_remote_copy(
            src_ref=qall_s.at[my_slot],
            dst_ref=qall_s.at[my_slot],
            send_sem=dq_send.at[d],
            recv_sem=dq_recv.at[my_slot],
            device_id=device(peer),
            device_id_type=MESH,
        )

    def dq_start(d, carry):
        dq_copy(d).start()
        return carry

    lax.fori_loop(1, count, dq_start, 0)

    for load in loads[2:5]:
        load.wait()
    own = pl.ds(n, n)
    rows = ext_s[pl.ds(TAIL, n), :]
    q_s[...] = (dot(rows, wq_s[...]) * factor).astype(BF16)
    k_s[own, :] = dot(rows, wk_s[...]).astype(BF16)
    v_s[own, :] = dot(rows, wv_s[...]).astype(BF16)

    def bias_of(start, size, valid_row):
        offset = (
            lax.broadcasted_iota(jnp.int32, (n, size), 1)
            - lax.broadcasted_iota(jnp.int32, (n, size), 0)
            + (start - n)
        )
        far = jnp.abs(offset).astype(F32) > reach_col
        gone = (valid_row < 0.5) & (offset != 0)
        bias_s[:, pl.ds(start, size)] = jnp.where(far | gone, FAR, 0.0)

    bias_of(n, n, sorted_valid[:1, :])

    lane = lax.broadcasted_iota(jnp.int32, (1, LANES), 1)
    first = jnp.where(lane < head_width, 1.0, 0.0)
    keep = (first.astype(BF16), (1.0 - first).astype(BF16))

    def own_pair(p, carry):
        cols = pl.ds(pl.multiple_of(p * LANES, LANES), LANES)
        qp, kp, vp = q_s[:, cols], k_s[own, cols], v_s[own, cols]
        for h in range(2):
            s = dot_nt(qp * keep[h], kp) + bias_s[:, own]
            m = jnp.max(s, axis=1, keepdims=True)
            weights = jnp.exp2(s - m).astype(BF16)
            acc_s[p, h] = dot(weights, vp * keep[h] + keep[1 - h])
            mx_s[p, h] = jnp.broadcast_to(m, (n, LANES))
        return carry

    lax.fori_loop(0, pairs, own_pair, 0, unroll=2)

    def split_heads(o0, o1):
        front = lane < head_width
        return (
            jnp.where(front, o0, o1),
            pltpu.roll(jnp.where(front, o1, o0), head_width, 1),
        )

    def place(side, start, size):
        there = pl.multiple_of(2 * side * n + start, half)
        rows = halo_s[side, pl.ds(pl.multiple_of(TAIL + start, TAIL), size), :]
        k_s[pl.ds(there, size), :] = dot(rows, wk_s[...]).astype(BF16)
        v_s[pl.ds(there, size), :] = dot(rows, wv_s[...]).astype(BF16)
        valid_at = pl.multiple_of((1 - side) * (n + TAIL), TAIL)
        valid_row = halo_s[side, pl.ds(valid_at, TAIL), pl.ds(pl.multiple_of(start, half), size)]
        bias_of(there, size, valid_row.astype(F32)[:1, :])

    def extended(p, h, here, span):
        cols = pl.ds(pl.multiple_of(p * LANES, LANES), LANES)
        s = dot_nt(q_s[here, cols] * keep[h], k_s[span, cols]) + bias_s[here, span]
        before = mx_s[p, h, here, :]
        m = jnp.maximum(before[:, :1], jnp.max(s, axis=1, keepdims=True))
        out = acc_s[p, h, here, :] * jnp.exp2(before - m)
        out += dot(jnp.exp2(s - m).astype(BF16), v_s[span, cols] * keep[h] + keep[1 - h])
        return out, m

    def tile(base, k, size=half):
        return pl.ds(pl.multiple_of(base + k * half, half), size)

    def carry_on(p, jobs):
        for here, span in jobs:
            for h in range(2):
                out, m = extended(p, h, here, span)
                acc_s[p, h, here, :] = out
                mx_s[p, h, here, :] = jnp.broadcast_to(m, out.shape)

    near_copy(near_side).wait_recv()
    place(near_side, 0, n)
    near_base, near_t = 2 * near_side * n, 1 - near_side

    def near_pair(p, carry):
        carry_on(
            p,
            (
                (tile(0, near_t), tile(near_base, near_t)),
                (tile(0, 1 - near_t), tile(near_base, 0, n)),
            ),
        )
        return carry

    lax.fori_loop(0, pairs, near_pair, 0, unroll=2)

    far_base, far_t = 2 * far_side * n, 1 - far_side
    far_copy(far_side, 0).wait_recv()
    place(far_side, far_t * half, half)

    def far_pair(p, carry):
        carry_on(p, ((pl.ds(0, n), tile(far_base, far_t)),))
        return carry

    lax.fori_loop(0, pairs, far_pair, 0, unroll=2)

    far_copy(far_side, 1).wait_recv()
    place(far_side, (1 - far_t) * half, half)

    def last_pair(p, carry):
        cols = pl.ds(pl.multiple_of(p * LANES, LANES), LANES)
        here = tile(0, far_t)
        value, total = split_heads(acc_s[p, 0, here, :], acc_s[p, 1, here, :])
        ctx_s[here, cols] = (value / total).astype(BF16)
        here = tile(0, 1 - far_t)
        span = tile(far_base, 1 - far_t)
        value, total = split_heads(
            extended(p, 0, here, span)[0], extended(p, 1, here, span)[0]
        )
        ctx_s[here, cols] = (value / total).astype(BF16)
        return carry

    lax.fori_loop(0, pairs, last_pair, 0, unroll=2)

    for load in loads[5:8]:
        load.wait()
    middle = rms_norm(
        dot(ctx_s[...], wo_s[...]) + ext_s[pl.ds(TAIL, n), :].astype(F32), gain1_ref[...]
    ).astype(BF16)
    ffn_s[...] = middle.astype(F32)
    hidden_width = up_s.shape[1]
    step = 512

    for c in range(hidden_width // step):
        hidden = gelu(dot(middle, up_s[:, pl.ds(c * step, step)])).astype(BF16)
        ffn_s[...] += dot(hidden, down_s[pl.ds(c * step, step), :])
    encoded = rms_norm(ffn_s[...], gain2_ref[...]).astype(BF16)
    enc_s[...] = encoded
    enc_copy = pltpu.make_async_copy(enc_s, enc_hbm, enc_sem)
    enc_copy.start()

    loads[8].wait()
    loads[9].wait()
    dk_s[...] = dot(encoded, dwk_s[...]).astype(BF16)
    dv_s[...] = dot(encoded, dwv_s[...]).astype(BF16)

    def dq_wait(d, carry):
        peer = lax.rem(me + d, count)
        slot = lax.rem(peer, n_query) * n_hit + lax.div(peer, n_query)
        pltpu.make_async_remote_copy(
            src_ref=qall_s.at[slot],
            dst_ref=qall_s.at[slot],
            send_sem=dq_send.at[d],
            recv_sem=dq_recv.at[slot],
            device_id=device(peer),
            device_id_type=MESH,
        ).wait_recv()
        return carry

    lax.fori_loop(1, count, dq_wait, 0)

    def partial(which):
        slots = pl.ds(which * n_hit, n_hit)

        for p in range(pairs):
            cols = pl.ds(p * LANES, LANES)
            qp = qall_s[slots, :, cols].reshape(part, LANES)
            kp, vp = dk_s[:, cols], dv_s[:, cols]
            outs, tops = [], []
            for h in range(2):
                s = dot_nt(qp * keep[h], kp)
                m = jnp.max(s, axis=1, keepdims=True)
                outs.append(dot(jnp.exp2(s - m).astype(BF16), vp * keep[h] + keep[1 - h]))
                tops.append(m)
            value, total = split_heads(*outs)
            o_s[:, cols] = value / total
            lse_s[:, cols] = jnp.where(lane < head_width, tops[0], tops[1]) + jnp.log2(total)

    column = lax.broadcasted_iota(jnp.int32, (width, LANES), 0)
    slot_of = lax.broadcasted_iota(jnp.int32, (width, LANES), 1)

    def packed(lse):
        total = jnp.zeros((lse.shape[0], LANES), F32)
        rest = lse
        for k in range(3):
            term = rest.astype(BF16)
            rest = rest - term.astype(F32)
            pick = jnp.where(column == (slot_of - k * HEADS) * head_width, 1.0, 0.0)
            total += dot(term, pick.astype(BF16))
        return total.astype(BF16)

    spread_row = lax.broadcasted_iota(jnp.int32, (LANES, width), 0)
    spread_col = lax.broadcasted_iota(jnp.int32, (LANES, width), 1)
    spread = jnp.zeros((LANES, width), F32)
    for k in range(3):
        low = (spread_row - k * HEADS) * head_width
        spread += jnp.where((spread_col >= low) & (spread_col < low + head_width), 1.0, 0.0)
    spread = spread.astype(BF16)

    partial(1 - core)
    pair_s[:, pl.ds(0, width)] = o_s[...].astype(BF16)
    pair_s[:, pl.ds(width, LANES)] = packed(lse_s[...])
    pair_copy = pltpu.make_async_remote_copy(
        src_ref=pair_s,
        dst_ref=pairin_s,
        send_sem=pair_send,
        recv_sem=pair_recv,
        device_id=(group, hit, 1 - core),
        device_id_type=MESH,
    )
    pair_copy.start()
    partial(core)
    pair_copy.wait_recv()
    lse_a, lse_b = lse_s[...], dot(pairin_s[:, pl.ds(width, LANES)], spread)
    top = jnp.maximum(lse_a, lse_b)
    wa, wb = jnp.exp2(lse_a - top), jnp.exp2(lse_b - top)
    total = wa + wb
    merged = (wa * o_s[...] + wb * pairin_s[:, pl.ds(0, width)].astype(F32)) / total
    msg_s[:, :, pl.ds(0, width)] = merged.astype(BF16).reshape(n_hit, owned, width)
    msg_s[:, :, pl.ds(width, LANES)] = packed(top + jnp.log2(total)).reshape(
        n_hit, owned, LANES
    )

    def msg_copy(d):
        peer = lax.rem(hit + d, n_hit)
        return pltpu.make_async_remote_copy(
            src_ref=msg_s.at[peer],
            dst_ref=msgin_s.at[hit],
            send_sem=msg_send.at[d],
            recv_sem=msg_recv.at[hit],
            device_id=(group, peer, core),
            device_id_type=MESH,
        )

    def msg_start(d, carry):
        msg_copy(d).start()
        return carry

    lax.fori_loop(1, n_hit, msg_start, 0)
    msgin_s[hit] = msg_s[hit]
    loads[10].wait()
    loads[11].wait()

    def msg_wait(d, carry):
        peer = lax.rem(hit + d, n_hit)
        pltpu.make_async_remote_copy(
            src_ref=msg_s.at[peer],
            dst_ref=msgin_s.at[peer],
            send_sem=msg_send.at[d],
            recv_sem=msg_recv.at[peer],
            device_id=(group, peer, core),
            device_id_type=MESH,
        ).wait_recv()
        return carry

    lax.fori_loop(1, n_hit, msg_wait, 0)
    values = msgin_s[:, :, pl.ds(0, width)].astype(F32)
    lse = dot(msgin_s[:, :, pl.ds(width, LANES)].reshape(part, LANES), spread)
    lse = lse.reshape(n_hit, owned, width)
    weights = jnp.exp2(lse - jnp.max(lse, axis=0, keepdims=True))
    cross = jnp.sum(weights * values, axis=0) / jnp.sum(weights, axis=0)
    res = dot(cross.astype(BF16), dwo_s[...]) + objq_ref[...].astype(F32)
    normed = rms_norm(res, dgain_ref[...]).astype(BF16)
    dec_ref[...] = dot(normed, out_s[...]).astype(BF16)

    far_copy(1 - core, 0).wait_send()
    far_copy(1 - core, 1).wait_send()
    near_copy(core).wait_send()

    def dq_sent(d, carry):
        dq_copy(d).wait_send()
        return carry

    lax.fori_loop(1, count, dq_sent, 0)
    pair_copy.wait_send()

    def msg_sent(d, carry):
        msg_copy(d).wait_send()
        return carry

    lax.fori_loop(1, n_hit, msg_sent, 0)
    enc_copy.wait()


def hand_over(enc_in, dec_in, enc_out, dec_out):
    enc_out[...] = enc_in[...]
    dec_out[...] = dec_in[...]


def on_device(
    n_hit,
    n_query,
    hits,
    order,
    valid,
    reach,
    enc_wq,
    enc_wk,
    enc_wv,
    enc_wo,
    enc_gain1,
    ffn_up,
    ffn_down,
    enc_gain2,
    object_queries,
    dec_wq,
    dec_wk,
    dec_wv,
    dec_wo,
    dec_gain,
    out_proj,
):
    n, width = hits.shape
    owned = object_queries.shape[0]
    hidden = ffn_up.shape[1]
    count = n_hit * n_query
    part = n_hit * owned
    pairs = width // LANES
    vmem = pl.BlockSpec(memory_space=pltpu.VMEM)
    anywhere = pl.BlockSpec(memory_space=pl.ANY)
    square = pltpu.VMEM((width, width), BF16)
    dma = pltpu.SemaphoreType.DMA
    raw = pl.pallas_call(
        functools.partial(kernel, n_hit, n_query),
        out_shape=(
            jax.ShapeDtypeStruct((n, width), BF16),
            jax.ShapeDtypeStruct((owned, width), BF16),
        ),
        in_specs=[vmem] * 7 + [anywhere] * 12,
        out_specs=(anywhere, vmem),
        scratch_shapes=[
            pltpu.VMEM((n, width), BF16),
            square,
            square,
            square,
            square,
            square,
            pltpu.VMEM((width, hidden), BF16),
            pltpu.VMEM((hidden, width), BF16),
            square,
            square,
            square,
            square,
            pltpu.VMEM((n + 2 * TAIL, width), BF16),
            pltpu.VMEM((2, n + 2 * TAIL, width), BF16),
            pltpu.VMEM((n, width), BF16),
            pltpu.VMEM((3 * n, width), BF16),
            pltpu.VMEM((3 * n, width), BF16),
            pltpu.VMEM((n, 3 * n), F32),
            pltpu.VMEM((pairs, 2, n, LANES), F32),
            pltpu.VMEM((pairs, 2, n, LANES), F32),
            pltpu.VMEM((n, width), BF16),
            pltpu.VMEM((n, width), F32),
            pltpu.VMEM((n, width), BF16),
            pltpu.VMEM((n, width), BF16),
            pltpu.VMEM((n, width), BF16),
            pltpu.VMEM((count, owned, width), BF16),
            pltpu.VMEM((part, width), F32),
            pltpu.VMEM((part, width), F32),
            pltpu.VMEM((part, width + LANES), BF16),
            pltpu.VMEM((part, width + LANES), BF16),
            pltpu.VMEM((n_hit, owned, width + LANES), BF16),
            pltpu.VMEM((n_hit, owned, width + LANES), BF16),
            dma((12,)),
            dma((3,)),
            dma((3,)),
            dma((count,)),
            dma((count,)),
            dma,
            dma,
            dma((n_hit,)),
            dma((n_hit,)),
            dma,
        ],
        compiler_params=pltpu.CompilerParams(
            collective_id=0, has_side_effects=True, vmem_limit_bytes=56 * 1024 * 1024
        ),
        name="track",
    )(
        order,
        valid.reshape(1, n),
        reach.reshape(1, n),
        enc_gain1.reshape(1, width),
        enc_gain2.reshape(1, width),
        dec_gain.reshape(1, width),
        object_queries,
        hits,
        enc_wq,
        enc_wk,
        enc_wv,
        dec_wq,
        enc_wo,
        ffn_up,
        ffn_down,
        dec_wk,
        dec_wv,
        dec_wo,
        out_proj,
    )
    return pl.pallas_call(
        hand_over,
        out_shape=tuple(jax.ShapeDtypeStruct(r.shape, r.dtype) for r in raw),
        in_specs=[vmem] * 2,
        out_specs=(vmem, vmem),
        name="hand_over",
    )(*raw)


def solution(mesh):
    split = P(("groups", "hit", "query"), None)
    flat = P(("groups", "hit", "query"))
    in_specs = (split, split, flat, flat) + (P(),) * 8 + (split,) + (P(),) * 6
    return jax.shard_map(
        functools.partial(on_device, mesh.shape["hit"], mesh.shape["query"]),
        mesh=mesh,
        in_specs=in_specs,
        out_specs=(split, split),
        check_vma=False,
    )
```
